256 devices in a mesh: rep: 4 (over y), ep: 64 (over z, x, core).
Axes of the slice: x: 4, y: 4, z: 8, core: 2. Of those that a mesh axis runs over, the one named last changes fastest.
Arguments:
- signal: bfloat16 [8192, 4096], P('ep', 'rep'), may hold values from -6 to 6
- routes: int32 [8192, 8], P('ep'), may hold values from 0 to 63, all different within a row; in each aligned block of 128 rows (0 to 127, 128 to 255, ...) at most 20 rows name the same one
- gates: float32 [8192, 8], P('ep'), may hold values from 0.05 to 0.5
- pairing: int32 [6144], P('ep'), may hold values from 0 to 31
- w_gate: bfloat16 [64, 4096, 768], P('ep', 'rep'), may hold values from -0.09375 to 0.09375
- w_up: bfloat16 [64, 4096, 768], P('ep', 'rep'), may hold values from -0.09375 to 0.09375
- w_down: bfloat16 [64, 768, 4096], P('ep', None, 'rep'), may hold values from -0.21875 to 0.21875
Outputs:
- mixed: bfloat16 [8192, 4096], P('ep', 'rep')
- grad_gate: bfloat16 [64, 4096, 768], P('ep', 'rep')
- grad_up: bfloat16 [64, 4096, 768], P('ep', 'rep')
- grad_down: bfloat16 [64, 768, 4096], P('ep', None, 'rep')
The draws below stay inside these ranges and needn't reach their ends.
Inputs may be any that keep to these rules, and one draw needn't show every extreme that they name: `routes`: each row names 8 different experts. In each owner's block of 128 rows no expert is named by more than 20 rows, a bound that some block reaches. A token row's pairing counts from the first context row of its own block.
All inputs are finite; a program needn't handle non-finite values.
Results may differ from the reference program's by a relative error of at most 0.01.
Values may be sent and summed in bfloat16 or wider, within the bound.
No kernel may reach another device: no remote copies, remote signals or barrier semaphores. Data moves between devices by JAX's collectives and lax.ppermute only.
A program may use at most 128 MiB of HBM per device.

```python
import math
import jax
import jax.numpy as jnp
import numpy as np
from jax import lax

D = 4096
HIDDEN_SIZE = 768
TOP = 8
TOK_DEV = 96
CTX_DEV = 32
ROW_DEV = 128
EXPERTS = 64
CAP = 20
SLOTS = 1280
ROWS = 8192
TOKENS = 6144
N_EP = 64


def plant(drawn, stream_key, smallest, top_value):
    spot = [jax.random.randint(jax.random.fold_in(stream_key, axis), (), 0, length) for axis, length in enumerate(drawn.shape)]
    longest = drawn.shape.index(max(drawn.shape))
    beside = spot[:longest] + [(spot[longest] + 1) % drawn.shape[longest]] + spot[longest + 1:]
    return drawn.at[tuple(spot)].set(smallest).at[tuple(beside)].set(top_value)


def block_scale(rng, extent, split, least, high):
    def one(axis_at, parts):
        heights = jax.random.uniform(jax.random.fold_in(jax.random.fold_in(rng, 6), axis_at), (parts,), jnp.float32, least / len(split), high / len(split))
        return jnp.repeat(jnp.exp(heights), extent[axis_at] // parts).reshape((-1,) + (1,) * (len(extent) - axis_at - 1))

    level = one(*split[0])
    for cut in split[1:]:
        level = level * one(*cut)
    return level


def deal_out(own_key, own, number, rows, number_of, top, bound, slope):
    sequence = jax.random.permutation(own_key, number_of)
    crowded, common = shares(number_of, rows * top, bound, slope, True), shares(number_of, rows * top, bound, slope, False)
    places = jnp.arange(number_of)

    def named(sizes, rotation):
        used = int((sizes > 0).sum())
        fixed = max(1, used // 4)
        shifted = fixed + (places - fixed + rotation * (used - fixed)) % max(1, number_of - fixed)
        return jnp.zeros((number_of,), jnp.int32).at[sequence[jnp.where(places < fixed, places, shifted)]].set(jnp.asarray(sizes, jnp.int32))

    sizes = jnp.where(number % 4 == 0, named(crowded, number // 4), named(common, number - number // 4 - 1))
    mixed = jax.random.permutation(jax.random.fold_in(own, 3), number_of)
    source_of, sink = mixed[0:number_of // 2 * 2:2], mixed[1:number_of // 2 * 2:2]
    slack = jnp.minimum(sizes[source_of] - 1, bound - sizes[sink]) // 2
    slack = jnp.where((source_of == sequence[0]) | (sink == sequence[0]) | (sizes[sink] == 0), 0, jnp.maximum(slack, 0))
    shifted = jax.random.randint(jax.random.fold_in(own, 4), (number_of // 2,), 0, 1 << 20) % (slack + 1)
    sizes = sizes.at[source_of].add(-shifted).at[sink].add(shifted)
    members = jnp.searchsorted(jnp.cumsum(sizes), jnp.arange(rows * top), side="right").astype(jnp.int32)
    grid = members.reshape(top, rows).T
    grid = grid[jax.random.permutation(jax.random.fold_in(own, 1), rows)]
    rotation = jax.random.randint(jax.random.fold_in(own, 2), (rows, 1), 0, top)
    return jnp.take_along_axis(grid, (jnp.arange(top)[None, :] + rotation) % top, axis=1)


def shares(number_of, total, bound, skew, full):
    weights = [(1 << 20) // math.isqrt(standing ** skew) + 1 for standing in range(1, number_of + 1)]
    largest = bound if full else min(bound, max(-(-total // number_of), total * weights[0] // sum(weights)))
    least = 1 if total - largest >= number_of - 1 else 0
    given, rest = [largest] + [least] * (number_of - 1), total - largest - least * (number_of - 1)
    while rest > 0:
        movable = [i for i in range(1, number_of) if given[i] < largest] or [i for i in range(1, number_of) if given[i] < bound]
        whole, remaining = sum([weights[i] for i in movable]), rest
        for i in movable:
            extra = min(bound - given[i], max(1, remaining * weights[i] // whole), rest)
            given[i] = given[i] + extra
            rest = rest - extra
    return np.array(given)


def gaussian(rng, shape, spread, limit, pieces=(), kind=jnp.bfloat16):
    result = spread * jax.random.normal(rng, shape, jnp.float32)
    if pieces:
        result = result * block_scale(rng, shape, pieces, -0.22, 0.18)
    return jnp.clip(result, -limit, limit).astype(kind)


def setup_inputs(seed: int = 0) -> dict:
    keys = jax.random.split(jax.random.key(seed), 8)
    signal = gaussian(keys[0], (ROWS, D), 1.0, 6.0, ((0, 64), (1, 4)))
    routes_keys = jax.random.split(jax.random.fold_in(keys[1], 1), ROWS // ROW_DEV)
    routes_turns = jax.random.permutation(jax.random.fold_in(keys[1], 3), ROWS // ROW_DEV)
    routes = jax.vmap(lambda own, number: deal_out(jax.random.fold_in(keys[1], 2), own, number, ROW_DEV, EXPERTS, TOP, CAP, 1))(routes_keys, routes_turns).reshape((ROWS, TOP))
    gates = jnp.clip(jnp.exp(math.log(0.5) - 2.3025851 * jax.random.uniform(keys[2], (ROWS, TOP), jnp.float32) ** block_scale(keys[2], (ROWS, TOP), ((0, 64),), -0.2, 0.2)), 0.05, 0.5)
    pairing = plant(jax.random.randint(keys[3], (TOKENS,), 0, CTX_DEV), jax.random.fold_in(keys[3], 1), 0, CTX_DEV - 1).astype(jnp.int32)
    w_gate = gaussian(keys[4], (EXPERTS, D, HIDDEN_SIZE), D ** -0.5, 0.09375, ((0, 64), (1, 4)))
    w_up = gaussian(keys[5], (EXPERTS, D, HIDDEN_SIZE), D ** -0.5, 0.09375, ((0, 64), (1, 4)))
    w_down = gaussian(keys[6], (EXPERTS, HIDDEN_SIZE, D), HIDDEN_SIZE ** -0.5, 0.21875, ((0, 64), (2, 4)))
    return dict(signal=signal, routes=routes, gates=gates, pairing=pairing, w_gate=w_gate, w_up=w_up, w_down=w_down)


epsilon = 1e-06

def route_slots(block_routes, capacity, experts):
    flat = block_routes.reshape(-1).astype(jnp.int32)
    onehot = (flat[:, None] == jnp.arange(experts, dtype=jnp.int32)[None, :]).astype(jnp.int32)
    position = lax.optimization_barrier(jnp.sum(jnp.cumsum(onehot, axis=0) * onehot, axis=1)) - 1
    return (flat, position.astype(jnp.int32))

def swish(gate, upper):
    return gate * jax.nn.sigmoid(gate) * upper

def row_gradient(combined, pair_block):
    squares = lax.optimization_barrier(jnp.sum(combined * combined, axis=1))
    scale = lax.rsqrt(squares / D + epsilon)
    normed = combined * scale[:, None]
    pair_table = (pair_block[:, None] == jnp.arange(CTX_DEV, dtype=jnp.int32)[None, :]).astype(jnp.float32)
    targets = jnp.dot(pair_table, normed[TOK_DEV:], precision=lax.Precision.HIGHEST)
    diff = normed[:TOK_DEV] - targets
    back = jnp.dot(pair_table.T, diff, precision=lax.Precision.HIGHEST)
    grad_normed = jnp.concatenate([diff, -back], axis=0) / TOK_DEV
    dots = lax.optimization_barrier(jnp.sum(grad_normed * normed, axis=1))
    return scale[:, None] * (grad_normed - normed * (dots / D)[:, None])

def reference(signal, routes, gates, pairing, w_gate, w_up, w_down):
    block_routes = routes.reshape(N_EP, ROW_DEV * TOP)
    experts_of, positions = jax.vmap(lambda blk: route_slots(blk, CAP, EXPERTS))(block_routes)
    block_index = jnp.arange(N_EP, dtype=jnp.int32)[:, None]
    global_slot = experts_of * SLOTS + block_index * CAP + positions
    row_index = block_index * ROW_DEV + (jnp.arange(ROW_DEV * TOP, dtype=jnp.int32) // TOP)[None, :]
    slot_row = jnp.full((EXPERTS * SLOTS,), ROWS, jnp.int32)
    slot_row = slot_row.at[global_slot.reshape(-1)].set(row_index.reshape(-1)).reshape(EXPERTS, SLOTS)
    padded = jnp.concatenate([signal, jnp.zeros((1, D), jnp.bfloat16)], axis=0)

    def expert_forward(inputs):
        rows_of, gate_weight, up_weight, down_weight = inputs
        arrived = padded[rows_of]
        gate = jnp.dot(arrived, gate_weight, preferred_element_type=jnp.float32)
        upper = jnp.dot(arrived, up_weight, preferred_element_type=jnp.float32)
        hidden = swish(gate, upper).astype(jnp.bfloat16)
        return jnp.dot(hidden, down_weight, preferred_element_type=jnp.float32).astype(jnp.bfloat16)
    outputs = lax.map(expert_forward, (slot_row, w_gate, w_up, w_down)).reshape(EXPERTS * SLOTS, D)

    def block_step(inputs):
        slot_block, gate_block, pair_block = inputs
        picked = outputs[slot_block].astype(jnp.float32).reshape(ROW_DEV, TOP, D)
        combined = lax.optimization_barrier(jnp.sum(picked * gate_block[:, :, None], axis=1))
        grad_rows = row_gradient(combined, pair_block)
        route_grad = (grad_rows[:, None, :] * gate_block[:, :, None]).astype(jnp.bfloat16)
        return (combined, route_grad.reshape(ROW_DEV * TOP, D))
    combined, route_grads = lax.map(block_step, (global_slot, gates.reshape(N_EP, ROW_DEV, TOP), pairing.reshape(N_EP, TOK_DEV)))
    grad_slots = jnp.zeros((EXPERTS * SLOTS, D), jnp.bfloat16)
    grad_slots = grad_slots.at[global_slot.reshape(-1)].set(route_grads.reshape(-1, D)).reshape(EXPERTS, SLOTS, D)

    def expert_backward(inputs):
        rows_of, grad_out, gate_weight, up_weight, down_weight = inputs
        arrived = padded[rows_of]
        gate = jnp.dot(arrived, gate_weight, preferred_element_type=jnp.float32)
        upper = jnp.dot(arrived, up_weight, preferred_element_type=jnp.float32)
        hidden = swish(gate, upper).astype(jnp.bfloat16)
        grad_down = jnp.dot(hidden.T, grad_out, preferred_element_type=jnp.float32)
        grad_hidden = jnp.dot(grad_out, down_weight.T, preferred_element_type=jnp.float32)
        sigma = jax.nn.sigmoid(gate)
        grad_gate_pre = (grad_hidden * upper * sigma * (1.0 + gate * (1.0 - sigma))).astype(jnp.bfloat16)
        grad_up_pre = (grad_hidden * gate * sigma).astype(jnp.bfloat16)
        grad_gate = jnp.dot(arrived.T, grad_gate_pre, preferred_element_type=jnp.float32)
        grad_upper = jnp.dot(arrived.T, grad_up_pre, preferred_element_type=jnp.float32)
        return (grad_gate.astype(jnp.bfloat16), grad_upper.astype(jnp.bfloat16), grad_down.astype(jnp.bfloat16))
    grad_gate, grad_upper, grad_down = lax.map(expert_backward, (slot_row, grad_slots, w_gate, w_up, w_down))
    mixed = combined.reshape(ROWS, D).astype(jnp.bfloat16)
    return (mixed, grad_gate, grad_upper, grad_down)
```

```python
import jax
import jax.numpy as jnp
from jax import lax
from jax.experimental import pallas as pl
from jax.experimental.pallas import tpu as pltpu
from jax.sharding import Mesh, PartitionSpec as P

D = 4096
TOP = 8
CAP = 20
NREP, NZ, NX, NC = 4, 8, 4, 2
PIECE = NZ * CAP

epsilon = 1e-06
bf16 = jnp.bfloat16
f32 = jnp.float32

NEAR = ((0, 0), (0, 1), (1, 0), (3, 0))
FAR = ((2, 0), (2, 1), (1, 1), (3, 1))
ALL = NEAR + FAR


def plane_shift(block, dx, dc):
    if dx == 0 and dc == 0:
        return block
    perm = [
        (a * NC + b, ((a + dx) % NX) * NC + (b + dc) % NC) for a in range(NX) for b in range(NC)
    ]
    return lax.ppermute(block, ("x", "c"), perm)


def rep_shift(block, step):
    return lax.ppermute(block, "rep", [(i, (i + step) % NREP) for i in range(NREP)])


def place_kernel(weighted, key_ref, gate_ref, rows_ref, *out_refs):
    rows = rows_ref[...]
    slots = lax.broadcasted_iota(jnp.int32, (PIECE, rows.shape[0]), 0).astype(f32)
    for i, out_ref in enumerate(out_refs):
        here = slots == key_ref[i : i + 1, :]
        weight = gate_ref[i : i + 1, :] if weighted else 1.0
        table = jnp.where(here, weight, 0.0).astype(bf16)
        out_ref[...] = jnp.dot(table, rows, preferred_element_type=f32).astype(bf16)


def place(keys, weights, rows, weighted):
    count, width = rows.shape
    return pl.pallas_call(
        lambda *refs: place_kernel(weighted, *refs),
        out_shape=[jax.ShapeDtypeStruct((PIECE, width), bf16)] * len(ALL),
        compiler_params=pltpu.CompilerParams(vmem_limit_bytes=40 * 1024 * 1024),
        cost_estimate=pl.CostEstimate(
            flops=2 * len(ALL) * PIECE * count * width, bytes_accessed=5 << 20, transcendentals=0
        ),
    )(keys, weights, rows)


def mix_kernel(key_ref, gate_ref, *refs):
    piece_refs, out_ref, held = refs[: len(ALL)], refs[len(ALL)], refs[len(ALL) + 1]
    half = len(ALL) // 2
    total = half * PIECE
    count = out_ref.shape[0]
    for i, ref in enumerate(piece_refs):
        held[i * PIECE : (i + 1) * PIECE, :] = ref[...]
    step = 256
    lanes = lax.broadcasted_iota(jnp.int32, (step, total), 1).astype(f32)
    for start in range(0, count, step):
        acc = None
        for group in range(2):
            table = jnp.zeros((step, total), f32)
            for i in range(half):
                j = group * half + i
                key = key_ref[start : start + step, j : j + 1] + float(i * PIECE)
                table = jnp.where(lanes == key, gate_ref[start : start + step, j : j + 1], table)
            part = jnp.dot(
                table.astype(bf16),
                held[group * total : (group + 1) * total, :],
                preferred_element_type=f32,
            )
            acc = part if acc is None else acc + part
        out_ref[start : start + step, :] = acc.astype(bf16)


def mix(key_rows, gate_rows, pieces):
    count = key_rows.shape[0]
    width = pieces[0].shape[1]
    return pl.pallas_call(
        mix_kernel,
        out_shape=jax.ShapeDtypeStruct((count, width), bf16),
        scratch_shapes=[pltpu.VMEM((len(ALL) * PIECE, width), bf16)],
        compiler_params=pltpu.CompilerParams(vmem_limit_bytes=48 * 1024 * 1024),
        cost_estimate=pl.CostEstimate(
            flops=2 * len(ALL) * PIECE * count * width, bytes_accessed=5 << 20, transcendentals=0
        ),
    )(key_rows, gate_rows, *pieces)


def route_tables(routes, gates):
    row_count = routes.shape[0]
    zi, xi, ci = lax.axis_index("z"), lax.axis_index("x"), lax.axis_index("c")
    dx = jnp.array([d[0] for d in ALL], jnp.int32)
    dc = jnp.array([d[1] for d in ALL], jnp.int32)
    within = ((xi + dx) % NX) * NC + (ci + dc) % NC
    expert = (jnp.arange(NZ, dtype=jnp.int32)[:, None] * (NX * NC) + within[None, :]).reshape(-1)
    hit = routes.T[:, None, :] == expert[None, :, None]
    named = jnp.any(hit, axis=0)
    gate = jnp.sum(jnp.where(hit, gates.T[:, None, :], 0.0), axis=0)
    order = jnp.arange(row_count, dtype=jnp.int32)
    earlier = (order[:, None] < order[None, :]).astype(bf16)
    position = jnp.dot(named.astype(bf16), earlier, preferred_element_type=f32)
    key = jnp.where(named, position * NZ + zi.astype(f32), -4096.0)
    return key, gate


def local(signal, routes, gates, pairing, w_gate, w_up, w_down):
    row_count = signal.shape[0]
    tokens = pairing.shape[0]
    contexts = row_count - tokens
    r = lax.axis_index("rep")
    both_weight = jnp.concatenate([w_gate[0], w_up[0]], axis=1)
    down_weight = w_down[0]
    hidden_width = down_weight.shape[0]

    plane_rows = lax.all_gather(signal, "z", axis=0, tiled=True)
    key, gate = route_tables(routes, gates)
    tables = jnp.concatenate(
        [key.reshape(NZ, len(ALL), row_count), gate.reshape(NZ, len(ALL), row_count)], axis=1
    )
    tables = lax.all_to_all(tables, "z", split_axis=0, concat_axis=0, tiled=True)
    flipped = tables.transpose(1, 0, 2).reshape(2 * len(ALL), NZ * row_count)
    keys, weights = flipped[: len(ALL)], flipped[len(ALL) :]
    key_rows, gate_rows = keys.T, weights.T

    def relative(pieces):
        stacked = jnp.stack(pieces)
        return [
            lax.dynamic_index_in_dim(stacked, (r + k) % NREP, 0, keepdims=False)
            for k in range(NREP)
        ]

    def absolute(pieces):
        stacked = jnp.stack(pieces)
        return [
            lax.dynamic_index_in_dim(stacked, (j - r) % NREP, 0, keepdims=False)
            for j in range(NREP)
        ]

    def rep_sum(parts):
        far = rep_shift(parts[2].astype(bf16), 2)
        right = rep_shift(parts[1].astype(bf16), 1)
        left = rep_shift(parts[3].astype(bf16), 3)
        return parts[0] + right.astype(f32) + left.astype(f32) + far.astype(f32)

    def rep_collect(own):
        far = rep_shift(own, 2)
        right = rep_shift(own, 3)
        left = rep_shift(own, 1)
        return [own, right, far, left]

    out = place(keys, weights, plane_rows, False)
    groups = ((0, NEAR), (len(NEAR), FAR))

    arrived, pre, hidden, returned = [], [], [], []
    for first, steps in groups:
        moved = [plane_shift(out[first + i], *d) for i, d in enumerate(steps)]
        arrived.append(relative(moved))
    for g in range(2):
        parts = [jnp.dot(a, both_weight, preferred_element_type=f32) for a in arrived[g]]
        own = rep_sum(parts)
        pre.append(own)
        gate_own, up_own = own[:, :hidden_width], own[:, hidden_width:]
        hidden.append(rep_collect((gate_own * jax.nn.sigmoid(gate_own) * up_own).astype(bf16)))
        rows = [
            jnp.dot(h, down_weight, preferred_element_type=f32).astype(bf16)
            for h in absolute(hidden[g])
        ]
        steps = groups[g][1]
        returned += [plane_shift(rows[i], (-d[0]) % NX, d[1]) for i, d in enumerate(steps)]

    partial = mix(key_rows, gate_rows, returned)
    mixed = lax.psum_scatter(partial, "z", scatter_dimension=0, tiled=True)

    combined = mixed.astype(f32)
    paired = pairing[:, None] == jnp.arange(contexts, dtype=jnp.int32)[None, :]
    pair_table = paired.astype(f32)
    target = jnp.dot(paired.astype(bf16), mixed[tokens:], preferred_element_type=f32)
    squares_part = jnp.sum(combined * combined, axis=1)
    cross_part = jnp.sum(combined[:tokens] * target, axis=1)
    sums = lax.psum(jnp.stack([squares_part, jnp.pad(cross_part, (0, contexts))]), "rep")
    squares, cross = sums[0], sums[1, :tokens]
    scale = lax.rsqrt(squares / D + epsilon)
    scale_target = jnp.sum(jnp.where(paired, scale[None, tokens:], 0.0), axis=1)
    own_norm = scale * scale * squares
    cross_norm = scale[:tokens] * scale_target * cross
    dots = (
        jnp.concatenate(
            [
                own_norm[:tokens] - cross_norm,
                jnp.sum(pair_table, axis=0) * own_norm[tokens:]
                - jnp.sum(jnp.where(paired, cross_norm[:, None], 0.0), axis=0),
            ]
        )
        / tokens
    )
    normed = combined * scale[:, None]
    diff = normed[:tokens] - target * scale_target[:, None]
    grad_normed = (
        jnp.concatenate(
            [diff, -jnp.dot(pair_table.T, diff, precision=lax.Precision.HIGHEST)], axis=0
        )
        / tokens
    )
    grad_rows = scale[:, None] * (grad_normed - normed * (dots / D)[:, None])

    plane_grads = lax.all_gather(grad_rows.astype(bf16), "z", axis=0, tiled=True)
    grad_out = place(keys, weights, plane_grads, True)
    grads, pre_grads = [], []
    for first, steps in groups:
        moved = [plane_shift(grad_out[first + i], *d) for i, d in enumerate(steps)]
        grads.append(relative(moved))
    for g in range(2):
        parts = [
            lax.dot_general(
                a, down_weight, (((1,), (1,)), ((), ())), preferred_element_type=f32
            )
            for a in grads[g]
        ]
        grad_hidden = rep_sum(parts)
        gate_own, up_own = pre[g][:, :hidden_width], pre[g][:, hidden_width:]
        sigma = jax.nn.sigmoid(gate_own)
        grad_gate_rows = grad_hidden * up_own * sigma * (1.0 + gate_own * (1.0 - sigma))
        grad_up_rows = grad_hidden * gate_own * sigma
        pre_grads.append(
            rep_collect(jnp.concatenate([grad_gate_rows, grad_up_rows], axis=1).astype(bf16))
        )

    def join(lists):
        return jnp.concatenate(lists[0] + lists[1], axis=0)

    over_rows = (((0,), (0,)), ((), ()))
    grad_down = lax.dot_general(
        join(hidden), join(grads), over_rows, preferred_element_type=f32
    ).astype(bf16)
    grad_both = lax.dot_general(
        join(arrived), join(pre_grads), over_rows, preferred_element_type=f32
    ).astype(bf16)
    return (
        mixed,
        grad_both[None, :, :hidden_width],
        grad_both[None, :, hidden_width:],
        grad_down[None],
    )


def solution(mesh):
    split = Mesh(mesh.devices.reshape(NREP, NZ, NX, NC), ("rep", "z", "x", "c"))
    ep = ("z", "x", "c")
    return jax.shard_map(
        local,
        mesh=split,
        in_specs=(
            P(ep, "rep"),
            P(ep, None),
            P(ep, None),
            P(ep),
            P(ep, "rep", None),
            P(ep, "rep", None),
            P(ep, None, "rep"),
        ),
        out_specs=(
            P(ep, "rep"),
            P(ep, "rep", None),
            P(ep, "rep", None),
            P(ep, None, "rep"),
        ),
        check_vma=False,
    )
```

```python
import jax
import jax.numpy as jnp
from jax import lax
from jax.experimental import pallas as pl
from jax.experimental.pallas import tpu as pltpu
from jax.sharding import Mesh, PartitionSpec as P

D = 4096
TOP = 8
CAP = 20
NREP, NZ, NX, NC = 4, 8, 4, 2
PIECE = NZ * CAP
TOK = 96

epsilon = 1e-06
bf16 = jnp.bfloat16
f32 = jnp.float32

NEAR = ((0, 0), (0, 1), (1, 0), (3, 0), (1, 1), (3, 1))
FAR = ((2, 0), (2, 1))
ALL = NEAR + FAR


def plane_shift(block, dx, dc):
    if dx == 0 and dc == 0:
        return block
    perm = [
        (a * NC + b, ((a + dx) % NX) * NC + (b + dc) % NC) for a in range(NX) for b in range(NC)
    ]
    return lax.ppermute(block, ("x", "c"), perm)


def rep_shift(block, step):
    return lax.ppermute(block, "rep", [(i, (i + step) % NREP) for i in range(NREP)])


def place_kernel(weighted, key_ref, gate_ref, rows_ref, *out_refs):
    rows = rows_ref[...]
    slots = lax.broadcasted_iota(jnp.int32, (PIECE, rows.shape[0]), 0).astype(f32)
    for i, out_ref in enumerate(out_refs):
        here = slots == key_ref[i : i + 1, :]
        weight = gate_ref[i : i + 1, :] if weighted else 1.0
        table = jnp.where(here, weight, 0.0).astype(bf16)
        out_ref[...] = jnp.dot(table, rows, preferred_element_type=f32).astype(bf16)


def place(keys, weights, rows, weighted):
    count, width = rows.shape
    return pl.pallas_call(
        lambda *refs: place_kernel(weighted, *refs),
        out_shape=[jax.ShapeDtypeStruct((PIECE, width), bf16)] * keys.shape[0],
        compiler_params=pltpu.CompilerParams(vmem_limit_bytes=40 * 1024 * 1024),
        cost_estimate=pl.CostEstimate(
            flops=2 * keys.shape[0] * PIECE * count * width,
            bytes_accessed=4 << 20,
            transcendentals=0,
        ),
    )(keys, weights, rows)


def gradient_kernel(line_ref, column_ref, rows_ref, out_ref):
    size = column_ref.shape[0]
    down = lax.broadcasted_iota(jnp.int32, (size, size), 0).astype(f32)
    across = lax.broadcasted_iota(jnp.int32, (size, size), 1).astype(f32)
    for b in range(NZ):
        scale_row, target_row = line_ref[8 * b : 8 * b + 1, :], line_ref[8 * b + 2 : 8 * b + 3, :]
        scale = column_ref[:, 8 * b : 8 * b + 1]
        diagonal = column_ref[:, 8 * b + 1 : 8 * b + 2]
        target = column_ref[:, 8 * b + 2 : 8 * b + 3]
        paired = (across == target) | (down == target_row)
        matrix = jnp.where(
            paired,
            -(scale * scale_row) * (1.0 / TOK),
            jnp.where(down == across, diagonal, 0.0),
        )
        rows = rows_ref[b * size : (b + 1) * size, :]
        acc = None
        for _ in range(3):
            term = matrix.astype(bf16)
            matrix = matrix - term.astype(f32)
            part = jnp.dot(term, rows, preferred_element_type=f32)
            acc = part if acc is None else acc + part
        out_ref[b * size : (b + 1) * size, :] = acc.astype(bf16)


def gradient(lines, columns, rows):
    return pl.pallas_call(
        gradient_kernel,
        out_shape=jax.ShapeDtypeStruct(rows.shape, bf16),
        compiler_params=pltpu.CompilerParams(vmem_limit_bytes=40 * 1024 * 1024),
        cost_estimate=pl.CostEstimate(
            flops=6 * rows.shape[0] * 128 * rows.shape[1],
            bytes_accessed=4 << 20,
            transcendentals=0,
        ),
    )(lines, columns, rows)


def mix_kernel(key_ref, gate_ref, *refs):
    piece_refs, out_ref, held = refs[: len(ALL)], refs[len(ALL)], refs[len(ALL) + 1]
    half = len(ALL) // 2
    total = half * PIECE
    count = out_ref.shape[0]
    for i, ref in enumerate(piece_refs):
        held[i * PIECE : (i + 1) * PIECE, :] = ref[...]
    step = 256
    lanes = lax.broadcasted_iota(jnp.int32, (step, total), 1).astype(f32)
    for start in range(0, count, step):
        acc = None
        for group in range(2):
            table = jnp.zeros((step, total), f32)
            for i in range(half):
                j = group * half + i
                key = key_ref[start : start + step, j : j + 1] + float(i * PIECE)
                table = jnp.where(lanes == key, gate_ref[start : start + step, j : j + 1], table)
            part = jnp.dot(
                table.astype(bf16),
                held[group * total : (group + 1) * total, :],
                preferred_element_type=f32,
            )
            acc = part if acc is None else acc + part
        out_ref[start : start + step, :] = acc.astype(bf16)


def mix(key_rows, gate_rows, pieces):
    count = key_rows.shape[0]
    width = pieces[0].shape[1]
    return pl.pallas_call(
        mix_kernel,
        out_shape=jax.ShapeDtypeStruct((count, width), bf16),
        scratch_shapes=[pltpu.VMEM((len(ALL) * PIECE, width), bf16)],
        compiler_params=pltpu.CompilerParams(vmem_limit_bytes=48 * 1024 * 1024),
        cost_estimate=pl.CostEstimate(
            flops=2 * len(ALL) * PIECE * count * width, bytes_accessed=5 << 20, transcendentals=0
        ),
    )(key_rows, gate_rows, *pieces)


def route_tables(routes, gates):
    row_count = routes.shape[0]
    zi, xi, ci = lax.axis_index("z"), lax.axis_index("x"), lax.axis_index("c")
    dx = jnp.array([d[0] for d in ALL], jnp.int32)
    dc = jnp.array([d[1] for d in ALL], jnp.int32)
    within = ((xi + dx) % NX) * NC + (ci + dc) % NC
    expert = (jnp.arange(NZ, dtype=jnp.int32)[:, None] * (NX * NC) + within[None, :]).reshape(-1)
    hit = routes.T[:, None, :] == expert[None, :, None]
    named = jnp.any(hit, axis=0)
    gate = jnp.sum(jnp.where(hit, gates.T[:, None, :], 0.0), axis=0)
    order = jnp.arange(row_count, dtype=jnp.int32)
    earlier = (order[:, None] < order[None, :]).astype(bf16)
    position = jnp.dot(named.astype(bf16), earlier, preferred_element_type=f32)
    key = jnp.where(named, position * NZ + zi.astype(f32), -4096.0)
    return key, gate


def local(signal, routes, gates, pairing, w_gate, w_up, w_down):
    row_count = signal.shape[0]
    tokens = pairing.shape[0]
    contexts = row_count - tokens
    near_count = len(NEAR)
    r = lax.axis_index("rep")
    both_weight = jnp.concatenate([w_gate[0], w_up[0]], axis=1)
    down_weight = w_down[0]
    hidden_width = down_weight.shape[0]

    plane_rows = lax.all_gather(signal, "z", axis=0, tiled=True)
    key, gate = route_tables(routes, gates)
    tables = jnp.concatenate(
        [key.reshape(NZ, len(ALL), row_count), gate.reshape(NZ, len(ALL), row_count)], axis=1
    )
    tables = lax.all_to_all(tables, "z", split_axis=0, concat_axis=0, tiled=True)
    flipped = tables.transpose(1, 0, 2).reshape(2 * len(ALL), NZ * row_count)
    keys, weights = flipped[: len(ALL)], flipped[len(ALL) :]
    key_rows, gate_rows = keys.T, weights.T

    def relative(pieces):
        whole = jnp.concatenate(pieces, axis=0)
        size = whole.shape[0] // NREP
        return whole, [
            lax.dynamic_slice_in_dim(whole, ((r + k) % NREP) * size, size, 0) for k in range(NREP)
        ]

    def absolute(pieces):
        size = pieces[0].shape[0]
        whole = jnp.zeros((NREP * size, pieces[0].shape[1]), pieces[0].dtype)
        for k, piece in enumerate(pieces):
            whole = lax.dynamic_update_slice_in_dim(whole, piece, ((r + k) % NREP) * size, 0)
        return whole

    def rep_send(parts):
        return (
            parts[0],
            rep_shift(parts[2].astype(bf16), 2),
            rep_shift(parts[1].astype(bf16), 1),
            rep_shift(parts[3].astype(bf16), 3),
        )

    def rep_total(sent):
        return sent[0] + sent[2].astype(f32) + sent[3].astype(f32) + sent[1].astype(f32)

    def rep_collect(own):
        far = rep_shift(own, 2)
        right = rep_shift(own, 3)
        left = rep_shift(own, 1)
        return [own, right, far, left]

    def dispatch(rows, weighted):
        close = place(keys[:near_count], weights[:near_count], rows, weighted)
        moved = [plane_shift(p, *d) for p, d in zip(close, NEAR)]
        moved, keys_far = lax.optimization_barrier((moved, keys[near_count:]))
        distant = place(keys_far, weights[near_count:], rows, weighted)
        return moved, [plane_shift(p, *d) for p, d in zip(distant, FAR)]

    def contract(hidden):
        return jnp.dot(hidden, down_weight, preferred_element_type=f32).astype(bf16)

    def give_back(rows, steps):
        return [
            plane_shift(rows[i * PIECE : (i + 1) * PIECE], (-d[0]) % NX, d[1])
            for i, d in enumerate(steps)
        ]

    def expand(pieces):
        return [jnp.dot(a, both_weight, preferred_element_type=f32) for a in pieces]

    def activate(own):
        gate_own, up_own = own[:, :hidden_width], own[:, hidden_width:]
        sigma = jax.nn.sigmoid(gate_own)
        hidden_own = (gate_own * sigma * up_own).astype(bf16)
        slopes = jnp.concatenate(
            [up_own * sigma * (1.0 + gate_own * (1.0 - sigma)), gate_own * sigma], axis=1
        ).astype(bf16)
        return hidden_own, slopes

    near, far = dispatch(plane_rows, False)
    near, near_parts = relative(near)
    hidden_near, slopes_near = activate(rep_total(rep_send(expand(near_parts))))
    hidden_near, far = lax.optimization_barrier((hidden_near, far))
    far, far_parts = relative(far)
    all_near = absolute(rep_collect(hidden_near))
    sent_far = rep_send(expand(far_parts))
    hidden_far, slopes_far = activate(rep_total(sent_far))
    rows_near = contract(all_near)
    pieces_far, rows_near = lax.optimization_barrier((rep_collect(hidden_far), rows_near))
    back_near = give_back(rows_near, NEAR)
    all_far = absolute(pieces_far)
    back_far = give_back(contract(all_far), FAR)

    slopes = jnp.concatenate([slopes_near, slopes_far], axis=0)
    partial = mix(key_rows, gate_rows, back_near + back_far)
    partial, slopes = lax.optimization_barrier((partial, slopes))
    gate_slopes = rep_collect(slopes[:, :hidden_width])
    mixed = lax.psum_scatter(partial, "z", scatter_dimension=0, tiled=True)
    mixed, gate_slopes = lax.optimization_barrier((mixed, gate_slopes))

    plane_mixed = lax.all_gather(mixed, "z", axis=0, tiled=True)
    combined = mixed.astype(f32)
    paired = pairing[:, None] == jnp.arange(contexts, dtype=jnp.int32)[None, :]
    target = jnp.dot(paired.astype(bf16), mixed[tokens:], preferred_element_type=f32)
    squares_part = jnp.sum(combined * combined, axis=1)
    cross_part = jnp.sum(combined[:tokens] * target, axis=1)
    sums = lax.psum(jnp.stack([squares_part, jnp.pad(cross_part, (0, contexts))]), "rep")
    sums, up_own = lax.optimization_barrier((sums, slopes[:, hidden_width:]))
    up_slopes = rep_collect(up_own)
    squares, cross = sums[0], sums[1, :tokens]
    scale = lax.rsqrt(squares / D + epsilon)
    scale_target = jnp.sum(jnp.where(paired, scale[None, tokens:], 0.0), axis=1)
    own_norm = scale * scale * squares
    cross_norm = scale[:tokens] * scale_target * cross
    members = jnp.sum(paired.astype(f32), axis=0)
    dots = jnp.concatenate(
        [
            own_norm[:tokens] - cross_norm,
            members * own_norm[tokens:]
            - jnp.sum(jnp.where(paired, cross_norm[:, None], 0.0), axis=0),
        ]
    )
    weight = jnp.concatenate([jnp.ones((tokens,), f32), members])
    diagonal = scale * scale * (weight - dots / D) / tokens
    pointer = jnp.pad(pairing.astype(f32) + tokens, (0, contexts), constant_values=-1.0)
    lines = jnp.pad(jnp.stack([scale, diagonal, pointer]), ((0, 5), (0, 0)))
    lines = lax.all_to_all(
        jnp.broadcast_to(lines[None], (NZ, 8, row_count)), "z", split_axis=0, concat_axis=0, tiled=True
    ).reshape(NZ * 8, row_count)

    plane_mixed, up_slopes = lax.optimization_barrier((plane_mixed, up_slopes))
    plane_grads = gradient(lines, lines.T, plane_mixed)
    grads_near, grads_far = dispatch(plane_grads, True)

    def back_through(pieces):
        return [
            lax.dot_general(
                a, down_weight, (((1,), (1,)), ((), ())), preferred_element_type=f32
            )
            for a in pieces
        ]

    grads_near, near_parts = relative(grads_near)
    grads_far, far_parts = relative(grads_far)
    sent_near = rep_send(back_through(near_parts))
    sent_far = rep_send(back_through(far_parts))
    grad_hidden = rep_collect(
        jnp.concatenate([rep_total(sent_near), rep_total(sent_far)], axis=0).astype(bf16)
    )

    def slope_product(slopes):
        size = near.shape[0] // NREP
        whole = [(h * s).astype(bf16) for h, s in zip(grad_hidden, slopes)]
        return jnp.concatenate(
            [absolute([w[:size] for w in whole]), absolute([w[size:] for w in whole])], axis=0
        )

    def weight_gradient(rows, row_grads):
        return lax.dot_general(
            rows, row_grads, (((0,), (0,)), ((), ())), preferred_element_type=f32
        ).astype(bf16)[None]

    arrived = jnp.concatenate([near, far], axis=0)
    grad_down = weight_gradient(
        jnp.concatenate([all_near, all_far], axis=0),
        jnp.concatenate([grads_near, grads_far], axis=0),
    )
    grad_gate = weight_gradient(arrived, slope_product(gate_slopes))
    grad_up = weight_gradient(arrived, slope_product(up_slopes))
    return (mixed, grad_gate, grad_up, grad_down)


def solution(mesh):
    split = Mesh(mesh.devices.reshape(NREP, NZ, NX, NC), ("rep", "z", "x", "c"))
    ep = ("z", "x", "c")
    return jax.shard_map(
        local,
        mesh=split,
        in_specs=(
            P(ep, "rep"),
            P(ep, None),
            P(ep, None),
            P(ep),
            P(ep, "rep", None),
            P(ep, "rep", None),
            P(ep, None, "rep"),
        ),
        out_specs=(
            P(ep, "rep"),
            P(ep, "rep", None),
            P(ep, "rep", None),
            P(ep, None, "rep"),
        ),
        check_vma=False,
    )
```

```python
import jax
import jax.numpy as jnp
from jax import lax
from jax.experimental import pallas as pl
from jax.experimental.pallas import tpu as pltpu
from jax.sharding import Mesh, PartitionSpec as P

D = 4096
TOP = 8
CAP = 20
NREP, NZ, NX, NC = 4, 8, 4, 2
PIECE = NZ * CAP
TOK = 96

epsilon = 1e-06
bf16 = jnp.bfloat16
f32 = jnp.float32

NEAR = ((0, 0), (0, 1), (1, 0), (3, 0), (1, 1), (3, 1))
FAR = ((2, 0), (2, 1))
ALL = NEAR + FAR


def plane_shift(block, dx, dc):
    if dx == 0 and dc == 0:
        return block
    perm = [
        (a * NC + b, ((a + dx) % NX) * NC + (b + dc) % NC) for a in range(NX) for b in range(NC)
    ]
    return lax.ppermute(block, ("x", "c"), perm)


def rep_shift(block, step):
    return lax.ppermute(block, "rep", [(i, (i + step) % NREP) for i in range(NREP)])


def place_kernel(weighted, key_ref, gate_ref, rows_ref, *out_refs):
    rows = rows_ref[...]
    slots = lax.broadcasted_iota(jnp.int32, (PIECE, rows.shape[0]), 0).astype(f32)
    for i, out_ref in enumerate(out_refs):
        here = slots == key_ref[i : i + 1, :]
        weight = gate_ref[i : i + 1, :] if weighted else 1.0
        table = jnp.where(here, weight, 0.0).astype(bf16)
        out_ref[...] = jnp.dot(table, rows, preferred_element_type=f32).astype(bf16)


def place(keys, weights, rows, weighted):
    count, width = rows.shape
    return pl.pallas_call(
        lambda *refs: place_kernel(weighted, *refs),
        out_shape=[jax.ShapeDtypeStruct((PIECE, width), bf16)] * keys.shape[0],
        compiler_params=pltpu.CompilerParams(vmem_limit_bytes=40 * 1024 * 1024),
        cost_estimate=pl.CostEstimate(
            flops=2 * keys.shape[0] * PIECE * count * width,
            bytes_accessed=4 << 20,
            transcendentals=0,
        ),
    )(keys, weights, rows)


def quarter(r_ref, k, size):
    return pl.multiple_of(lax.rem(r_ref[0] + k, NREP) * size, 16)


def spread_kernel(count, dims, r_ref, weight_ref, *refs):
    piece_refs, whole_ref, out_refs = refs[:count], refs[count], refs[count + 1 :]
    for i, ref in enumerate(piece_refs):
        whole_ref[i * PIECE : (i + 1) * PIECE, :] = ref[...]
    size = whole_ref.shape[0] // NREP
    weight = weight_ref[...]
    for k, out_ref in enumerate(out_refs):
        rows = whole_ref[pl.ds(quarter(r_ref, k, size), size), :]
        part = lax.dot_general(rows, weight, (dims, ((), ())), preferred_element_type=f32)
        out_ref[...] = part.astype(out_ref.dtype)


def spread(rank, weight, pieces, dims):
    count, width = len(pieces), pieces[0].shape[1]
    out_width = weight.shape[1 - dims[1][0]]
    size = count * PIECE // NREP
    part = lambda dtype: jax.ShapeDtypeStruct((size, out_width), dtype)
    whole, *parts = pl.pallas_call(
        lambda *refs: spread_kernel(count, dims, *refs),
        out_shape=[jax.ShapeDtypeStruct((count * PIECE, width), bf16), part(f32)]
        + [part(bf16)] * (NREP - 1),
        in_specs=[pl.BlockSpec(memory_space=pltpu.SMEM)]
        + [pl.BlockSpec(memory_space=pltpu.VMEM)] * (1 + count),
        compiler_params=pltpu.CompilerParams(vmem_limit_bytes=40 * 1024 * 1024),
        cost_estimate=pl.CostEstimate(
            flops=2 * count * PIECE * width * out_width, bytes_accessed=8 << 20, transcendentals=0
        ),
    )(rank, weight, *pieces)
    return whole, parts


def contract_kernel(near, r_ref, weight_ref, *refs):
    part_refs, whole_ref, out_refs = refs[:NREP], refs[NREP], refs[NREP + 1 :]
    join_quarters(near, r_ref, part_refs, whole_ref)
    weight = weight_ref[...]
    for i, out_ref in enumerate(out_refs):
        rows = whole_ref[i * PIECE : (i + 1) * PIECE, :]
        out_ref[...] = jnp.dot(rows, weight, preferred_element_type=f32).astype(bf16)


def join_quarters(near, r_ref, parts, whole_ref):
    far = parts[0].shape[0] - near
    for k, part in enumerate(parts):
        whole_ref[pl.ds(quarter(r_ref, k, near), near), :] = part[:near, :]
        place_at = pl.multiple_of(NREP * near + quarter(r_ref, k, far), 16)
        whole_ref[pl.ds(place_at, far), :] = part[near:, :]


def contract(rank, near, weight, parts):
    rows, width = NREP * parts[0].shape[0], parts[0].shape[1]
    whole, *out = pl.pallas_call(
        lambda *refs: contract_kernel(near, *refs),
        out_shape=[jax.ShapeDtypeStruct((rows, width), bf16)]
        + [jax.ShapeDtypeStruct((PIECE, weight.shape[1]), bf16)] * len(ALL),
        in_specs=[pl.BlockSpec(memory_space=pltpu.SMEM)]
        + [pl.BlockSpec(memory_space=pltpu.VMEM)] * (1 + NREP),
        compiler_params=pltpu.CompilerParams(vmem_limit_bytes=40 * 1024 * 1024),
        cost_estimate=pl.CostEstimate(
            flops=2 * rows * width * weight.shape[1], bytes_accessed=8 << 20, transcendentals=0
        ),
    )(rank, weight, *parts)
    return whole, out


def slope_kernel(near, r_ref, *refs):
    grad_refs, out_refs = refs[:NREP], refs[3 * NREP :]
    for j, out_ref in enumerate(out_refs):
        slope_refs = refs[(1 + j) * NREP : (2 + j) * NREP]
        parts = [
            (g[...].astype(f32) * s[...].astype(f32)).astype(bf16)
            for g, s in zip(grad_refs, slope_refs)
        ]
        join_quarters(near, r_ref, parts, out_ref)


def slope_products(rank, near, grads, gate_slopes, up_slopes):
    shape = jax.ShapeDtypeStruct((NREP * grads[0].shape[0], grads[0].shape[1]), bf16)
    return pl.pallas_call(
        lambda *refs: slope_kernel(near, *refs),
        out_shape=[shape, shape],
        in_specs=[pl.BlockSpec(memory_space=pltpu.SMEM)]
        + [pl.BlockSpec(memory_space=pltpu.VMEM)] * (3 * NREP),
        compiler_params=pltpu.CompilerParams(vmem_limit_bytes=40 * 1024 * 1024),
        cost_estimate=pl.CostEstimate(flops=4 << 20, bytes_accessed=10 << 20, transcendentals=0),
    )(rank, *grads, *gate_slopes, *up_slopes)


def gradient_kernel(line_ref, column_ref, rows_ref, out_ref):
    size = column_ref.shape[0]
    down = lax.broadcasted_iota(jnp.int32, (size, size), 0).astype(f32)
    across = lax.broadcasted_iota(jnp.int32, (size, size), 1).astype(f32)
    for b in range(NZ):
        scale_row, target_row = line_ref[8 * b : 8 * b + 1, :], line_ref[8 * b + 2 : 8 * b + 3, :]
        scale = column_ref[:, 8 * b : 8 * b + 1]
        diagonal = column_ref[:, 8 * b + 1 : 8 * b + 2]
        target = column_ref[:, 8 * b + 2 : 8 * b + 3]
        paired = (across == target) | (down == target_row)
        matrix = jnp.where(
            paired,
            -(scale * scale_row) * (1.0 / TOK),
            jnp.where(down == across, diagonal, 0.0),
        )
        rows = rows_ref[b * size : (b + 1) * size, :]
        acc = None
        for _ in range(3):
            term = matrix.astype(bf16)
            matrix = matrix - term.astype(f32)
            part = jnp.dot(term, rows, preferred_element_type=f32)
            acc = part if acc is None else acc + part
        out_ref[b * size : (b + 1) * size, :] = acc.astype(bf16)


def gradient(lines, columns, rows):
    return pl.pallas_call(
        gradient_kernel,
        out_shape=jax.ShapeDtypeStruct(rows.shape, bf16),
        compiler_params=pltpu.CompilerParams(vmem_limit_bytes=40 * 1024 * 1024),
        cost_estimate=pl.CostEstimate(
            flops=6 * rows.shape[0] * 128 * rows.shape[1],
            bytes_accessed=4 << 20,
            transcendentals=0,
        ),
    )(lines, columns, rows)


def mix_kernel(key_ref, gate_ref, *refs):
    piece_refs, out_ref, held = refs[: len(ALL)], refs[len(ALL)], refs[len(ALL) + 1]
    half = len(ALL) // 2
    total = half * PIECE
    count = out_ref.shape[0]
    for i, ref in enumerate(piece_refs):
        held[i * PIECE : (i + 1) * PIECE, :] = ref[...]
    step = 256
    lanes = lax.broadcasted_iota(jnp.int32, (step, total), 1).astype(f32)
    for start in range(0, count, step):
        acc = None
        for group in range(2):
            table = jnp.zeros((step, total), f32)
            for i in range(half):
                j = group * half + i
                key = key_ref[start : start + step, j : j + 1] + float(i * PIECE)
                table = jnp.where(lanes == key, gate_ref[start : start + step, j : j + 1], table)
            part = jnp.dot(
                table.astype(bf16),
                held[group * total : (group + 1) * total, :],
                preferred_element_type=f32,
            )
            acc = part if acc is None else acc + part
        out_ref[start : start + step, :] = acc.astype(bf16)


def mix(key_rows, gate_rows, pieces):
    count = key_rows.shape[0]
    width = pieces[0].shape[1]
    return pl.pallas_call(
        mix_kernel,
        out_shape=jax.ShapeDtypeStruct((count, width), bf16),
        scratch_shapes=[pltpu.VMEM((len(ALL) * PIECE, width), bf16)],
        compiler_params=pltpu.CompilerParams(vmem_limit_bytes=48 * 1024 * 1024),
        cost_estimate=pl.CostEstimate(
            flops=2 * len(ALL) * PIECE * count * width, bytes_accessed=5 << 20, transcendentals=0
        ),
    )(key_rows, gate_rows, *pieces)


def route_tables(routes, gates):
    row_count = routes.shape[0]
    zi, xi, ci = lax.axis_index("z"), lax.axis_index("x"), lax.axis_index("c")
    dx = jnp.array([d[0] for d in ALL], jnp.int32)
    dc = jnp.array([d[1] for d in ALL], jnp.int32)
    within = ((xi + dx) % NX) * NC + (ci + dc) % NC
    expert = (jnp.arange(NZ, dtype=jnp.int32)[:, None] * (NX * NC) + within[None, :]).reshape(-1)
    hit = routes.T[:, None, :] == expert[None, :, None]
    named = jnp.any(hit, axis=0)
    gate = jnp.sum(jnp.where(hit, gates.T[:, None, :], 0.0), axis=0)
    order = jnp.arange(row_count, dtype=jnp.int32)
    earlier = (order[:, None] < order[None, :]).astype(bf16)
    position = jnp.dot(named.astype(bf16), earlier, preferred_element_type=f32)
    key = jnp.where(named, position * NZ + zi.astype(f32), -4096.0)
    return key, gate


def local(signal, routes, gates, pairing, w_gate, w_up, w_down):
    row_count = signal.shape[0]
    tokens = pairing.shape[0]
    contexts = row_count - tokens
    near_count = len(NEAR)
    r = lax.axis_index("rep")
    both_weight = jnp.concatenate([w_gate[0], w_up[0]], axis=1)
    down_weight = w_down[0]
    hidden_width = down_weight.shape[0]

    plane_rows = lax.all_gather(signal, "z", axis=0, tiled=True)
    key, gate = route_tables(routes, gates)
    tables = jnp.concatenate(
        [key.reshape(NZ, len(ALL), row_count), gate.reshape(NZ, len(ALL), row_count)], axis=1
    )
    tables = lax.all_to_all(tables, "z", split_axis=0, concat_axis=0, tiled=True)
    flipped = tables.transpose(1, 0, 2).reshape(2 * len(ALL), NZ * row_count)
    keys, weights = flipped[: len(ALL)], flipped[len(ALL) :]
    key_rows, gate_rows = keys.T, weights.T

    def rep_send(parts):
        return (
            parts[0],
            rep_shift(parts[2], 2),
            rep_shift(parts[1], 1),
            rep_shift(parts[3], 3),
        )

    def rep_total(sent):
        return sent[0] + sent[2].astype(f32) + sent[3].astype(f32) + sent[1].astype(f32)

    def rep_collect(own):
        far = rep_shift(own, 2)
        right = rep_shift(own, 3)
        left = rep_shift(own, 1)
        return [own, right, far, left]

    def close_rows(rows, weighted):
        pieces = place(keys[: len(NEAR)], weights[: len(NEAR)], rows, weighted)
        return [plane_shift(p, *d) for p, d in zip(pieces, NEAR)]

    def distant_rows(rows, weighted, after):
        late_keys, after = lax.optimization_barrier((keys[len(NEAR) :], after))
        pieces = place(late_keys, weights[len(NEAR) :], rows, weighted)
        return [plane_shift(p, *d) for p, d in zip(pieces, FAR)], after

    def activate(own):
        gate_own, up_own = own[:, :hidden_width], own[:, hidden_width:]
        sigma = jax.nn.sigmoid(gate_own)
        hidden_own = (gate_own * sigma * up_own).astype(bf16)
        slopes = jnp.concatenate(
            [up_own * sigma * (1.0 + gate_own * (1.0 - sigma)), gate_own * sigma], axis=1
        ).astype(bf16)
        return hidden_own, slopes

    rank = r.reshape(1)
    near, parts_near = spread(rank, both_weight, close_rows(plane_rows, False), ((1,), (0,)))
    far, parts_near = distant_rows(plane_rows, False, parts_near)
    sent_near = rep_send(parts_near)
    first_near, far = lax.optimization_barrier((sent_near[2], far))
    own_near = rep_total((sent_near[0], sent_near[1], first_near, sent_near[3]))
    far, parts_far = spread(rank, both_weight, far, ((1,), (0,)))
    own_far = rep_total(rep_send(parts_far))
    near_size = own_near.shape[0]
    hidden, slopes = activate(jnp.concatenate([own_near, own_far], axis=0))
    hidden, rows_out = contract(rank, near_size, down_weight, rep_collect(hidden))
    returned = [plane_shift(p, (-d[0]) % NX, d[1]) for p, d in zip(rows_out, ALL)]

    partial = mix(key_rows, gate_rows, returned)
    partial, slopes = lax.optimization_barrier((partial, slopes))
    gate_slopes = rep_collect(slopes[:, :hidden_width])
    mixed = lax.psum_scatter(partial, "z", scatter_dimension=0, tiled=True)
    mixed, gate_slopes = lax.optimization_barrier((mixed, gate_slopes))

    plane_mixed = lax.all_gather(mixed, "z", axis=0, tiled=True)
    combined = mixed.astype(f32)
    paired = pairing[:, None] == jnp.arange(contexts, dtype=jnp.int32)[None, :]
    target = jnp.dot(paired.astype(bf16), mixed[tokens:], preferred_element_type=f32)
    squares_part = jnp.sum(combined * combined, axis=1)
    cross_part = jnp.sum(combined[:tokens] * target, axis=1)
    sums = lax.psum(jnp.stack([squares_part, jnp.pad(cross_part, (0, contexts))]), "rep")
    sums, up_own = lax.optimization_barrier((sums, slopes[:, hidden_width:]))
    up_slopes = rep_collect(up_own)
    squares, cross = sums[0], sums[1, :tokens]
    scale = lax.rsqrt(squares / D + epsilon)
    scale_target = jnp.sum(jnp.where(paired, scale[None, tokens:], 0.0), axis=1)
    own_norm = scale * scale * squares
    cross_norm = scale[:tokens] * scale_target * cross
    members = jnp.sum(paired.astype(f32), axis=0)
    dots = jnp.concatenate(
        [
            own_norm[:tokens] - cross_norm,
            members * own_norm[tokens:]
            - jnp.sum(jnp.where(paired, cross_norm[:, None], 0.0), axis=0),
        ]
    )
    weight = jnp.concatenate([jnp.ones((tokens,), f32), members])
    diagonal = scale * scale * (weight - dots / D) / tokens
    pointer = jnp.pad(pairing.astype(f32) + tokens, (0, contexts), constant_values=-1.0)
    lines = jnp.pad(jnp.stack([scale, diagonal, pointer]), ((0, 5), (0, 0)))
    lines = lax.all_to_all(
        jnp.broadcast_to(lines[None], (NZ, 8, row_count)), "z", split_axis=0, concat_axis=0, tiled=True
    ).reshape(NZ * 8, row_count)

    plane_mixed, up_slopes = lax.optimization_barrier((plane_mixed, up_slopes))
    plane_grads = gradient(lines, lines.T, plane_mixed)
    grads_near = close_rows(plane_grads, True)
    grads_far, grads_near = distant_rows(plane_grads, True, grads_near)

    grads_near, parts_near = spread(rank, down_weight, grads_near, ((1,), (1,)))
    sent_near = rep_send(parts_near)
    grads_far, parts_far = spread(rank, down_weight, grads_far, ((1,), (1,)))
    sent_far = rep_send(parts_far)
    grad_hidden = rep_collect(
        jnp.concatenate([rep_total(sent_near), rep_total(sent_far)], axis=0).astype(bf16)
    )
    gate_grads, up_grads = slope_products(rank, near_size, grad_hidden, gate_slopes, up_slopes)

    def weight_gradient(rows, row_grads):
        return lax.dot_general(
            rows, row_grads, (((0,), (0,)), ((), ())), preferred_element_type=f32
        ).astype(bf16)[None]

    arrived = jnp.concatenate([near, far], axis=0)
    grad_down = weight_gradient(hidden, jnp.concatenate([grads_near, grads_far], axis=0))
    grad_gate = weight_gradient(arrived, gate_grads)
    grad_up = weight_gradient(arrived, up_grads)
    return (mixed, grad_gate, grad_up, grad_down)


def solution(mesh):
    split = Mesh(mesh.devices.reshape(NREP, NZ, NX, NC), ("rep", "z", "x", "c"))
    ep = ("z", "x", "c")
    return jax.shard_map(
        local,
        mesh=split,
        in_specs=(
            P(ep, "rep"),
            P(ep, None),
            P(ep, None),
            P(ep),
            P(ep, "rep", None),
            P(ep, "rep", None),
            P(ep, None, "rep"),
        ),
        out_specs=(
            P(ep, "rep"),
            P(ep, "rep", None),
            P(ep, "rep", None),
            P(ep, None, "rep"),
        ),
        check_vma=False,
    )
```

```python
import jax
import jax.numpy as jnp
from jax import lax
from jax.experimental import pallas as pl
from jax.experimental.pallas import tpu as pltpu
from jax.sharding import Mesh, PartitionSpec as P

D = 4096
TOP = 8
CAP = 20
NREP, NZ, NX, NC = 4, 8, 4, 2
PIECE = NZ * CAP
TOK = 96

epsilon = 1e-06
bf16 = jnp.bfloat16
f32 = jnp.float32

NEAR = ((0, 0), (0, 1), (1, 0), (3, 0), (1, 1), (3, 1))
FAR = ((2, 0), (2, 1))
ALL = NEAR + FAR


def plane_shift(block, dx, dc):
    if dx == 0 and dc == 0:
        return block
    perm = [
        (a * NC + b, ((a + dx) % NX) * NC + (b + dc) % NC) for a in range(NX) for b in range(NC)
    ]
    return lax.ppermute(block, ("x", "c"), perm)


def rep_shift(block, step):
    return lax.ppermute(block, "rep", [(i, (i + step) % NREP) for i in range(NREP)])


def place_kernel(weighted, key_ref, gate_ref, rows_ref, *out_refs):
    rows = rows_ref[...]
    slots = lax.broadcasted_iota(jnp.int32, (PIECE, rows.shape[0]), 0).astype(f32)
    for i, out_ref in enumerate(out_refs):
        here = slots == key_ref[i : i + 1, :]
        weight = gate_ref[i : i + 1, :] if weighted else 1.0
        table = jnp.where(here, weight, 0.0).astype(bf16)
        out_ref[...] = jnp.dot(table, rows, preferred_element_type=f32).astype(bf16)


def place(keys, weights, rows, weighted):
    count, width = rows.shape
    return pl.pallas_call(
        lambda *refs: place_kernel(weighted, *refs),
        out_shape=[jax.ShapeDtypeStruct((PIECE, width), bf16)] * keys.shape[0],
        in_specs=[pl.BlockSpec(memory_space=pltpu.VMEM)] * 3,
        out_specs=[pl.BlockSpec(memory_space=pltpu.VMEM)] * keys.shape[0],
        compiler_params=pltpu.CompilerParams(vmem_limit_bytes=40 * 1024 * 1024),
        cost_estimate=pl.CostEstimate(
            flops=2 * keys.shape[0] * PIECE * count * width,
            bytes_accessed=4 << 20,
            transcendentals=0,
        ),
    )(keys, weights, rows)


def quarter(r_ref, k, size):
    return pl.multiple_of(lax.rem(r_ref[0] + k, NREP) * size, 16)


def spread_kernel(count, dims, r_ref, weight_ref, *refs):
    piece_refs, whole_ref, out_refs = refs[:count], refs[count], refs[count + 1 :]
    for i, ref in enumerate(piece_refs):
        whole_ref[i * PIECE : (i + 1) * PIECE, :] = ref[...]
    size = whole_ref.shape[0] // NREP
    weight = weight_ref[...]
    for k, out_ref in enumerate(out_refs):
        rows = whole_ref[pl.ds(quarter(r_ref, k, size), size), :]
        part = lax.dot_general(rows, weight, (dims, ((), ())), preferred_element_type=f32)
        out_ref[...] = part.astype(out_ref.dtype)


def spread(rank, weight, pieces, dims):
    count, width = len(pieces), pieces[0].shape[1]
    out_width = weight.shape[1 - dims[1][0]]
    size = count * PIECE // NREP
    part = lambda dtype: jax.ShapeDtypeStruct((size, out_width), dtype)
    whole, *parts = pl.pallas_call(
        lambda *refs: spread_kernel(count, dims, *refs),
        out_shape=[jax.ShapeDtypeStruct((count * PIECE, width), bf16), part(f32)]
        + [part(bf16)] * (NREP - 1),
        in_specs=[pl.BlockSpec(memory_space=pltpu.SMEM)]
        + [pl.BlockSpec(memory_space=pltpu.VMEM)] * (1 + count),
        out_specs=[pl.BlockSpec(memory_space=pltpu.VMEM)] * (1 + NREP),
        compiler_params=pltpu.CompilerParams(vmem_limit_bytes=40 * 1024 * 1024),
        cost_estimate=pl.CostEstimate(
            flops=2 * count * PIECE * width * out_width, bytes_accessed=8 << 20, transcendentals=0
        ),
    )(rank, weight, *pieces)
    return whole, parts


def contract_kernel(near, r_ref, weight_ref, *refs):
    part_refs, whole_ref, out_refs = refs[:NREP], refs[NREP], refs[NREP + 1 :]
    join_quarters(near, r_ref, part_refs, whole_ref)
    weight = weight_ref[...]
    for i, out_ref in enumerate(out_refs):
        rows = whole_ref[i * PIECE : (i + 1) * PIECE, :]
        out_ref[...] = jnp.dot(rows, weight, preferred_element_type=f32).astype(bf16)


def join_quarters(near, r_ref, parts, whole_ref):
    far = parts[0].shape[0] - near
    for k, part in enumerate(parts):
        whole_ref[pl.ds(quarter(r_ref, k, near), near), :] = part[:near, :]
        place_at = pl.multiple_of(NREP * near + quarter(r_ref, k, far), 16)
        whole_ref[pl.ds(place_at, far), :] = part[near:, :]


def contract(rank, near, weight, parts):
    rows, width = NREP * parts[0].shape[0], parts[0].shape[1]
    whole, *out = pl.pallas_call(
        lambda *refs: contract_kernel(near, *refs),
        out_shape=[jax.ShapeDtypeStruct((rows, width), bf16)]
        + [jax.ShapeDtypeStruct((PIECE, weight.shape[1]), bf16)] * len(ALL),
        in_specs=[pl.BlockSpec(memory_space=pltpu.SMEM)]
        + [pl.BlockSpec(memory_space=pltpu.VMEM)] * (1 + NREP),
        out_specs=[pl.BlockSpec(memory_space=pltpu.VMEM)] * (1 + len(ALL)),
        compiler_params=pltpu.CompilerParams(vmem_limit_bytes=40 * 1024 * 1024),
        cost_estimate=pl.CostEstimate(
            flops=2 * rows * width * weight.shape[1], bytes_accessed=8 << 20, transcendentals=0
        ),
    )(rank, weight, *parts)
    return whole, out


def slope_kernel(near, r_ref, *refs):
    grad_refs, out_refs = refs[:NREP], refs[3 * NREP :]
    for j, out_ref in enumerate(out_refs):
        slope_refs = refs[(1 + j) * NREP : (2 + j) * NREP]
        parts = [
            (g[...].astype(f32) * s[...].astype(f32)).astype(bf16)
            for g, s in zip(grad_refs, slope_refs)
        ]
        join_quarters(near, r_ref, parts, out_ref)


def slope_products(rank, near, grads, gate_slopes, up_slopes):
    shape = jax.ShapeDtypeStruct((NREP * grads[0].shape[0], grads[0].shape[1]), bf16)
    return pl.pallas_call(
        lambda *refs: slope_kernel(near, *refs),
        out_shape=[shape, shape],
        in_specs=[pl.BlockSpec(memory_space=pltpu.SMEM)]
        + [pl.BlockSpec(memory_space=pltpu.VMEM)] * (3 * NREP),
        compiler_params=pltpu.CompilerParams(vmem_limit_bytes=40 * 1024 * 1024),
        cost_estimate=pl.CostEstimate(flops=4 << 20, bytes_accessed=10 << 20, transcendentals=0),
    )(rank, *grads, *gate_slopes, *up_slopes)


def gradient_kernel(line_ref, column_ref, rows_ref, out_ref):
    size = column_ref.shape[0]
    down = lax.broadcasted_iota(jnp.int32, (size, size), 0).astype(f32)
    across = lax.broadcasted_iota(jnp.int32, (size, size), 1).astype(f32)
    for b in range(NZ):
        scale_row, target_row = line_ref[8 * b : 8 * b + 1, :], line_ref[8 * b + 2 : 8 * b + 3, :]
        scale = column_ref[:, 8 * b : 8 * b + 1]
        diagonal = column_ref[:, 8 * b + 1 : 8 * b + 2]
        target = column_ref[:, 8 * b + 2 : 8 * b + 3]
        paired = (across == target) | (down == target_row)
        matrix = jnp.where(
            paired,
            -(scale * scale_row) * (1.0 / TOK),
            jnp.where(down == across, diagonal, 0.0),
        )
        rows = rows_ref[b * size : (b + 1) * size, :]
        acc = None
        for _ in range(3):
            term = matrix.astype(bf16)
            matrix = matrix - term.astype(f32)
            part = jnp.dot(term, rows, preferred_element_type=f32)
            acc = part if acc is None else acc + part
        out_ref[b * size : (b + 1) * size, :] = acc.astype(bf16)


def gradient(lines, columns, rows):
    return pl.pallas_call(
        gradient_kernel,
        out_shape=jax.ShapeDtypeStruct(rows.shape, bf16),
        compiler_params=pltpu.CompilerParams(vmem_limit_bytes=40 * 1024 * 1024),
        cost_estimate=pl.CostEstimate(
            flops=6 * rows.shape[0] * 128 * rows.shape[1],
            bytes_accessed=4 << 20,
            transcendentals=0,
        ),
    )(lines, columns, rows)


def mix_kernel(first, key_ref, gate_ref, *refs):
    half = len(ALL) // 2
    piece_refs, earlier, out_ref, held = refs[:half], refs[half:-2], refs[-2], refs[-1]
    step = 128
    for i, ref in enumerate(piece_refs):
        held[i * PIECE : (i + 1) * PIECE, :] = ref[...]
    lanes = lax.broadcasted_iota(jnp.int32, (step, half * PIECE), 1).astype(f32)
    for start in range(0, out_ref.shape[0], step):
        rows = slice(start, start + step)
        table = jnp.zeros((step, half * PIECE), f32)
        for i in range(half):
            j = first + i
            key = key_ref[rows, j : j + 1] + float(i * PIECE)
            table = jnp.where(lanes == key, gate_ref[rows, j : j + 1], table)
        part = jnp.dot(table.astype(bf16), held[...], preferred_element_type=f32)
        for ref in earlier:
            part = part + ref[rows, :]
        out_ref[rows, :] = part.astype(out_ref.dtype)


def mix(key_rows, gate_rows, first, pieces, earlier=()):
    count = key_rows.shape[0]
    width = pieces[0].shape[1]
    return pl.pallas_call(
        lambda *refs: mix_kernel(first, *refs),
        out_shape=jax.ShapeDtypeStruct((count, width), bf16 if earlier else f32),
        scratch_shapes=[pltpu.VMEM((len(pieces) * PIECE, width), bf16)],
        compiler_params=pltpu.CompilerParams(vmem_limit_bytes=48 * 1024 * 1024),
        cost_estimate=pl.CostEstimate(
            flops=2 * len(pieces) * PIECE * count * width,
            bytes_accessed=7 << 20,
            transcendentals=0,
        ),
    )(key_rows, gate_rows, *pieces, *earlier)


def route_tables(routes, gates):
    row_count = routes.shape[0]
    zi, xi, ci = lax.axis_index("z"), lax.axis_index("x"), lax.axis_index("c")
    dx = jnp.array([d[0] for d in ALL], jnp.int32)
    dc = jnp.array([d[1] for d in ALL], jnp.int32)
    within = ((xi + dx) % NX) * NC + (ci + dc) % NC
    expert = (jnp.arange(NZ, dtype=jnp.int32)[:, None] * (NX * NC) + within[None, :]).reshape(-1)
    hit = routes.T[:, None, :] == expert[None, :, None]
    named = jnp.any(hit, axis=0)
    gate = jnp.sum(jnp.where(hit, gates.T[:, None, :], 0.0), axis=0)
    order = jnp.arange(row_count, dtype=jnp.int32)
    earlier = (order[:, None] < order[None, :]).astype(bf16)
    position = jnp.dot(named.astype(bf16), earlier, preferred_element_type=f32)
    key = jnp.where(named, position * NZ + zi.astype(f32), -4096.0)
    return key, gate


def local(signal, routes, gates, pairing, w_gate, w_up, w_down):
    row_count = signal.shape[0]
    tokens = pairing.shape[0]
    contexts = row_count - tokens
    near_count = len(NEAR)
    r = lax.axis_index("rep")
    both_weight = jnp.concatenate([w_gate[0], w_up[0]], axis=1)
    down_weight = w_down[0]
    hidden_width = down_weight.shape[0]

    plane_rows = lax.all_gather(signal, "z", axis=0, tiled=True)
    key, gate = route_tables(routes, gates)
    tables = jnp.concatenate(
        [key.reshape(NZ, len(ALL), row_count), gate.reshape(NZ, len(ALL), row_count)], axis=1
    )
    tables = lax.all_to_all(tables, "z", split_axis=0, concat_axis=0, tiled=True)
    flipped = tables.transpose(1, 0, 2).reshape(2 * len(ALL), NZ * row_count)
    keys, weights = flipped[: len(ALL)], flipped[len(ALL) :]
    key_rows, gate_rows = keys.T, weights.T

    def rep_send(parts):
        return (
            parts[0],
            rep_shift(parts[2], 2),
            rep_shift(parts[1], 1),
            rep_shift(parts[3], 3),
        )

    def rep_total(sent):
        return sent[0] + sent[2].astype(f32) + sent[3].astype(f32) + sent[1].astype(f32)

    def rep_collect(own):
        far = rep_shift(own, 2)
        right = rep_shift(own, 3)
        left = rep_shift(own, 1)
        return [own, right, far, left]

    def close_rows(rows, weighted):
        pieces = place(keys[: len(NEAR)], weights[: len(NEAR)], rows, weighted)
        return [plane_shift(p, *d) for p, d in zip(pieces, NEAR)]

    def distant_rows(rows, weighted, after):
        late_keys, after = lax.optimization_barrier((keys[len(NEAR) :], after))
        pieces = place(late_keys, weights[len(NEAR) :], rows, weighted)
        return [plane_shift(p, *d) for p, d in zip(pieces, FAR)], after

    def activate(own):
        gate_own, up_own = own[:, :hidden_width], own[:, hidden_width:]
        sigma = jax.nn.sigmoid(gate_own)
        hidden_own = (gate_own * sigma * up_own).astype(bf16)
        slopes = jnp.concatenate(
            [up_own * sigma * (1.0 + gate_own * (1.0 - sigma)), gate_own * sigma], axis=1
        ).astype(bf16)
        return hidden_own, slopes

    rank = r.reshape(1)
    near, parts_near = spread(rank, both_weight, close_rows(plane_rows, False), ((1,), (0,)))
    far, parts_near = distant_rows(plane_rows, False, parts_near)
    sent_near = rep_send(parts_near)
    first_near, far = lax.optimization_barrier((sent_near[2], far))
    own_near = rep_total((sent_near[0], sent_near[1], first_near, sent_near[3]))
    far, parts_far = spread(rank, both_weight, far, ((1,), (0,)))
    own_far = rep_total(rep_send(parts_far))
    near_size = own_near.shape[0]
    hidden, slopes = activate(jnp.concatenate([own_near, own_far], axis=0))
    hidden, rows_out = contract(rank, near_size, down_weight, rep_collect(hidden))
    returned = [plane_shift(p, (-d[0]) % NX, d[1]) for p, d in zip(rows_out, ALL)]

    half = len(ALL) // 2
    partial = mix(key_rows, gate_rows, 0, returned[:half])
    partial = mix(key_rows, gate_rows, half, returned[half:], (partial,))
    partial, slopes = lax.optimization_barrier((partial, slopes))
    gate_slopes = rep_collect(slopes[:, :hidden_width])
    mixed = lax.psum_scatter(partial, "z", scatter_dimension=0, tiled=True)
    mixed, gate_slopes = lax.optimization_barrier((mixed, gate_slopes))

    plane_mixed = lax.all_gather(mixed, "z", axis=0, tiled=True)
    combined = mixed.astype(f32)
    paired = pairing[:, None] == jnp.arange(contexts, dtype=jnp.int32)[None, :]
    target = jnp.dot(paired.astype(bf16), mixed[tokens:], preferred_element_type=f32)
    squares_part = jnp.sum(combined * combined, axis=1)
    cross_part = jnp.sum(combined[:tokens] * target, axis=1)
    sums = lax.psum(jnp.stack([squares_part, jnp.pad(cross_part, (0, contexts))]), "rep")
    sums, up_own = lax.optimization_barrier((sums, slopes[:, hidden_width:]))
    up_slopes = rep_collect(up_own)
    squares, cross = sums[0], sums[1, :tokens]
    scale = lax.rsqrt(squares / D + epsilon)
    scale_target = jnp.sum(jnp.where(paired, scale[None, tokens:], 0.0), axis=1)
    own_norm = scale * scale * squares
    cross_norm = scale[:tokens] * scale_target * cross
    members = jnp.sum(paired.astype(f32), axis=0)
    dots = jnp.concatenate(
        [
            own_norm[:tokens] - cross_norm,
            members * own_norm[tokens:]
            - jnp.sum(jnp.where(paired, cross_norm[:, None], 0.0), axis=0),
        ]
    )
    weight = jnp.concatenate([jnp.ones((tokens,), f32), members])
    diagonal = scale * scale * (weight - dots / D) / tokens
    pointer = jnp.pad(pairing.astype(f32) + tokens, (0, contexts), constant_values=-1.0)
    lines = jnp.pad(jnp.stack([scale, diagonal, pointer]), ((0, 5), (0, 0)))
    lines = lax.all_to_all(
        jnp.broadcast_to(lines[None], (NZ, 8, row_count)), "z", split_axis=0, concat_axis=0, tiled=True
    ).reshape(NZ * 8, row_count)

    plane_mixed, up_slopes = lax.optimization_barrier((plane_mixed, up_slopes))
    plane_grads = gradient(lines, lines.T, plane_mixed)
    grads_near = close_rows(plane_grads, True)
    grads_far, grads_near = distant_rows(plane_grads, True, grads_near)

    grads_near, parts_near = spread(rank, down_weight, grads_near, ((1,), (1,)))
    sent_near = rep_send(parts_near)
    grads_far, parts_far = spread(rank, down_weight, grads_far, ((1,), (1,)))
    sent_far = rep_send(parts_far)
    grad_hidden = rep_collect(
        jnp.concatenate([rep_total(sent_near), rep_total(sent_far)], axis=0).astype(bf16)
    )
    gate_grads, up_grads = slope_products(rank, near_size, grad_hidden, gate_slopes, up_slopes)

    def weight_gradient(rows, row_grads):
        return lax.dot_general(
            rows, row_grads, (((0,), (0,)), ((), ())), preferred_element_type=f32
        ).astype(bf16)[None]

    arrived = jnp.concatenate([near, far], axis=0)
    grad_down = weight_gradient(hidden, jnp.concatenate([grads_near, grads_far], axis=0))
    grad_gate = weight_gradient(arrived, gate_grads)
    grad_up = weight_gradient(arrived, up_grads)
    return (mixed, grad_gate, grad_up, grad_down)


def solution(mesh):
    split = Mesh(mesh.devices.reshape(NREP, NZ, NX, NC), ("rep", "z", "x", "c"))
    ep = ("z", "x", "c")
    return jax.shard_map(
        local,
        mesh=split,
        in_specs=(
            P(ep, "rep"),
            P(ep, None),
            P(ep, None),
            P(ep),
            P(ep, "rep", None),
            P(ep, "rep", None),
            P(ep, None, "rep"),
        ),
        out_specs=(
            P(ep, "rep"),
            P(ep, "rep", None),
            P(ep, "rep", None),
            P(ep, None, "rep"),
        ),
        check_vma=False,
    )
```
